32 devices in a mesh: seq: 16 (over z, y, core), tensor: 2 (over x).
Axes of the slice: x: 2, y: 2, z: 4, core: 2. Of those that a mesh axis runs over, the one named last changes fastest.
Arguments:
- features: bfloat16 [2048, 3072], P('seq', 'tensor'), may hold values from -6 to 6
- gain: float32 [3072], replicated, may hold values from 0.1 to 1.9
- w_qkv: bfloat16 [3072, 3, 3072], P(None, None, 'tensor'), may hold values from -0.109375 to 0.109375
- rope_factors: float32 [48], replicated, may hold values from 1 to 64
- cache_len: int32 [4], replicated, may hold values from 1 to 12288, as said below
- cache_kv: bfloat16 [192, 128, 2, 3072], P('seq', None, None, 'tensor'), may hold values from -405 to 405, as said below
- block_owner: int32 [192], P('seq'), may hold values from 0 to 4, as said below
- block_base: int32 [192], P('seq'), may hold values from 0 to 12160, as said below
Outputs:
- attended: bfloat16 [2048, 3072], P('seq', 'tensor')
- new_kv: bfloat16 [2048, 2, 3072], P('seq', None, 'tensor')
The draws below stay inside these ranges and needn't reach their ends.
Inputs may be any that keep to these rules, and one draw needn't show every extreme that they name: `cache_len`: one request has exactly 12288 cached tokens; the others have between 1 and 3072. `block_owner`: request r owns exactly ceil(cache_len[r] / 128) blocks, placed anywhere in the pool; 4 marks a free block, and some blocks are free. `block_base`: the blocks of request r carry the bases 0, 128, 256, ... below cache_len[r], each once; free blocks carry 0. `cache_kv`: stored keys are already rotated.
All inputs are finite; a program needn't handle non-finite values.
Results may differ from the reference program's by a relative error of at most 0.014.
The reference program's roundings to bfloat16 on the way (of `normed`) count: a program that leaves them out, or rounds other values in their place, can miss the bound.
Values may be sent and summed in bfloat16 or wider, within the bound.
A program may use at most 384 MiB of HBM per device.

```python
import math
import jax
import jax.numpy as jnp
from jax import lax

D = 3072
HEADS = 32
HD = 96
REQ = 4
BLK = 128
TOKENS = 2048
NEW = 512
NBLK = 192
CACHE_MAX = 12288
OTHER = 3072


def cache_layout(key):
    base_key = jax.random.fold_in(key, 11)
    pick_key, shift_key, size_key, shuffle_key = jax.random.split(base_key, 4)
    longest = jax.random.randint(pick_key, (), 0, REQ)
    shifts = jax.random.randint(shift_key, (REQ,), 0, 4)
    ceilings = jnp.right_shift(jnp.full((REQ,), OTHER, jnp.int32), shifts.astype(jnp.int32))
    others = jax.random.randint(size_key, (REQ,), 1, ceilings + 1)
    lengths = jnp.where(jnp.arange(REQ) == longest, CACHE_MAX, others).astype(jnp.int32)
    counts = (lengths + BLK - 1) // BLK
    closing = jnp.cumsum(counts)
    opening = closing - counts
    slot_ids = jnp.arange(NBLK, dtype=jnp.int32)
    owners = jnp.sum((slot_ids[:, None] >= closing[None, :]).astype(jnp.int32), axis=1).astype(jnp.int32)
    clamped = jnp.minimum(owners, REQ - 1)
    offsets = jnp.where(owners < REQ, (slot_ids - opening[clamped]) * BLK, 0).astype(jnp.int32)
    shuffle = jax.random.permutation(shuffle_key, NBLK)
    owner_array = jnp.zeros((NBLK,), jnp.int32).at[shuffle].set(owners)
    base_array = jnp.zeros((NBLK,), jnp.int32).at[shuffle].set(offsets)
    return (lengths, owner_array, base_array)


def draw_cache_len(key, part):
    return cache_layout(key)[0]


def draw_block_owner(key, part):
    return cache_layout(key)[1]


def draw_block_base(key, part):
    return cache_layout(key)[2]


def draw_cache_kv(key, part):
    value_key = jax.random.fold_in(jax.random.fold_in(key, 23), 0)
    entries = jnp.clip(jax.random.normal(value_key, (NBLK, BLK, 2, HEADS * HD), jnp.float32), -5.0, 5.0)
    return entries.astype(jnp.bfloat16)


def steps_of(rng, dims, shards, low, largest):
    level = 1.0
    for axis_at, shards_of in shards:
        steps = jax.random.uniform(jax.random.fold_in(jax.random.fold_in(rng, 6), axis_at), (shards_of,), jnp.float32, low / len(shards), largest / len(shards))
        level = level * jnp.repeat(jnp.exp(steps), dims[axis_at] // shards_of).reshape((-1,) + (1,) * (len(dims) - 1 - axis_at))
    return level


def scatter_about(rng, shape, deviation, limit, shards=(), held_as=jnp.bfloat16):
    values = deviation * jax.random.normal(rng, shape, jnp.float32)
    if shards:
        values = values * steps_of(rng, shape, shards, -0.22, 0.18)
    return jnp.clip(values, -limit, limit).astype(held_as)


def setup_inputs(seed: int = 0) -> dict:
    key_of = jax.random.split(jax.random.key(seed), 9)
    features = scatter_about(key_of[0], (TOKENS, D), 1.0, 6.0, ((0, 16), (1, 2)))
    gain = jnp.clip(1.0 + 0.18 * jax.random.normal(key_of[1], (D,), jnp.float32), 0.1, 1.9)
    w_qkv = scatter_about(key_of[2], (D, 3, HEADS * HD), D ** -0.5, 0.109375, ((2, 2),))
    rope_factors = jnp.clip(jnp.exp(jax.random.uniform(key_of[3], (HD // 2,), jnp.float32, math.log(1.0), math.log(64.0))), 1.0, 64.0)
    cache_len = draw_cache_len(jax.random.fold_in(key_of[8], 71), 0)
    cache_kv = draw_cache_kv(jax.random.fold_in(key_of[8], 71), 0)
    block_owner = draw_block_owner(jax.random.fold_in(key_of[8], 71), 0)
    block_base = draw_block_base(jax.random.fold_in(key_of[8], 71), 0)
    return dict(features=features, gain=gain, w_qkv=w_qkv, rope_factors=rope_factors, cache_len=cache_len, cache_kv=cache_kv, block_owner=block_owner, block_base=block_base)


EPSILON = 1e-05
NEGATIVE = -1e+30
MSCALE = 1.1902380714238083

def rotate(vectors, angles):
    half_dim = vectors.shape[-1] // 2
    front_half = vectors[..., :half_dim]
    back_half = vectors[..., half_dim:]
    cosine = jnp.cos(angles) * MSCALE
    sine_part = jnp.sin(angles) * MSCALE
    return jnp.concatenate([front_half * cosine - back_half * sine_part, back_half * cosine + front_half * sine_part], axis=-1)

def pick_row(array, where_at):
    return lax.dynamic_index_in_dim(array, where_at, 0, keepdims=False)

def put_row(array, update, where_at):
    return lax.dynamic_update_index_in_dim(array, update, where_at, 0)

def reference(features, gain, w_qkv, rope_factors, cache_len, cache_kv, block_owner, block_base):
    wide_x = features.astype(jnp.float32)
    normed = (wide_x * lax.rsqrt(lax.optimization_barrier(jnp.mean(wide_x * wide_x, axis=1, keepdims=True)) + EPSILON) * gain).astype(jnp.bfloat16)
    projected = jnp.einsum('td,dcf->tcf', normed.astype(jnp.float32), w_qkv.astype(jnp.float32))
    row_ids = jnp.arange(TOKENS, dtype=jnp.int32)
    positions = cache_len[row_ids // NEW] + row_ids % NEW
    inv_freq = 1.0 / (rope_factors * jnp.power(10000.0, jnp.arange(HD // 2, dtype=jnp.float32) * 2.0 / HD))
    angles = positions.astype(jnp.float32)[:, None, None] * inv_freq[None, None, :]
    shaped = projected.reshape(TOKENS, 3, HEADS, HD)
    queries = (rotate(shaped[:, 0], angles) * HD ** (-0.5)).astype(jnp.bfloat16)
    new_keys = rotate(shaped[:, 1], angles).astype(jnp.bfloat16)
    new_values = shaped[:, 2].astype(jnp.bfloat16)
    new_kv = jnp.stack([new_keys.reshape(TOKENS, HEADS * HD), new_values.reshape(TOKENS, HEADS * HD)], axis=1)
    query_req = queries.reshape(REQ, NEW, HEADS, HD)
    key_req = new_keys.reshape(REQ, NEW, HEADS, HD)
    value_req = new_values.reshape(REQ, NEW, HEADS, HD)
    own_pos = positions.reshape(REQ, NEW)
    causal = own_pos[:, None, :] <= own_pos[:, :, None]
    cache_keys = cache_kv[:, :, 0].reshape(NBLK, BLK, HEADS, HD)
    cache_values = cache_kv[:, :, 1].reshape(NBLK, BLK, HEADS, HD)
    clamped = jnp.minimum(block_owner, REQ - 1)
    bound_len = jnp.where(block_owner < REQ, cache_len[clamped], 0)
    usable = block_base[:, None] + jnp.arange(BLK, dtype=jnp.int32)[None, :] < bound_len[:, None]

    def one_head(head_id):
        head_q = lax.dynamic_index_in_dim(query_req, head_id, 2, keepdims=False)
        head_k = lax.dynamic_index_in_dim(key_req, head_id, 2, keepdims=False)
        head_v = lax.dynamic_index_in_dim(value_req, head_id, 2, keepdims=False)
        block_k = lax.dynamic_index_in_dim(cache_keys, head_id, 2, keepdims=False)
        block_v = lax.dynamic_index_in_dim(cache_values, head_id, 2, keepdims=False)
        new_scores = jnp.einsum('rnd,rkd->rnk', head_q.astype(jnp.float32), head_k.astype(jnp.float32))
        maxima = lax.optimization_barrier(jnp.max(jnp.where(causal, new_scores, NEGATIVE), axis=2))

        def first_step(running, paired):
            keys_b, usable_b, owner_b = paired
            scores = jnp.dot(pick_row(head_q, owner_b), keys_b.T, preferred_element_type=jnp.float32)
            block_max = lax.optimization_barrier(jnp.max(jnp.where(usable_b[None, :], scores, NEGATIVE), axis=1))
            return (put_row(running, jnp.maximum(pick_row(running, owner_b), block_max), owner_b), None)
        maxima = lax.scan(first_step, maxima, (block_k, usable, clamped))[0]
        weight = jnp.where(causal, jnp.exp(new_scores - maxima[:, :, None]), 0.0)
        rounded = lax.optimization_barrier(weight.astype(jnp.bfloat16))
        numerator = jnp.einsum('rnk,rkd->rnd', rounded.astype(jnp.float32), head_v.astype(jnp.float32))
        denominator = lax.optimization_barrier(jnp.sum(weight, axis=2))

        def second_step(running, paired):
            keys_b, values_b, usable_b, owner_b = paired
            numer_now, denom_now = running
            scores = jnp.dot(pick_row(head_q, owner_b), keys_b.T, preferred_element_type=jnp.float32)
            block_weight = jnp.where(usable_b[None, :], jnp.exp(scores - pick_row(maxima, owner_b)[:, None]), 0.0)
            term = jnp.dot(block_weight.astype(jnp.bfloat16), values_b, preferred_element_type=jnp.float32)
            numer_now = put_row(numer_now, pick_row(numer_now, owner_b) + term, owner_b)
            denom_now = put_row(denom_now, pick_row(denom_now, owner_b) + lax.optimization_barrier(jnp.sum(block_weight, axis=1)), owner_b)
            return ((numer_now, denom_now), None)
        numerator, denominator = lax.scan(second_step, (numerator, denominator), (block_k, block_v, usable, clamped))[0]
        return (numerator / denominator[:, :, None]).astype(jnp.bfloat16)
    per_head = lax.map(one_head, jnp.arange(HEADS, dtype=jnp.int32))
    attended = per_head.transpose(1, 2, 0, 3).reshape(TOKENS, HEADS * HD)
    return (attended, new_kv)
```

```python
import functools
import jax
import jax.numpy as jnp
from jax import lax
from jax.experimental import pallas as pl
from jax.experimental.pallas import tpu as pltpu
from jax.sharding import PartitionSpec as P

EPSILON = 1e-05
FLOOR = -1e30
MASKED = -2e30
MSCALE = 1.1902380714238083
GROUP = 4


def rotate_rows(vectors, cosine, sine):
    half = vectors.shape[1] // 2
    front, back = vectors[:, :half], vectors[:, half:]
    return jnp.concatenate([front * cosine - back * sine, back * cosine + front * sine], axis=1)


def attend_kernel(
    owner_ref, bound_ref, place_ref, first_ref,
    q_ref, k_ref, v_ref, nk_ref, nv_ref, out_ref, stat_ref, acc, peak, total,
    *, requests, per_request, head_dim,
):
    rows = q_ref.shape[2]
    blocks, slots = k_ref.shape[0], k_ref.shape[1]
    width = per_request * rows
    acc[...] = jnp.zeros_like(acc)
    peak[...] = jnp.full_like(peak, FLOOR)
    total[...] = jnp.zeros_like(total)

    def step(request, keys, values, mask):
        for head in range(GROUP):
            span = slice(head * head_dim, (head + 1) * head_dim)
            queries = jnp.concatenate(
                [q_ref[request * per_request + c, span, :] for c in range(per_request)], axis=1
            )
            scores = jnp.dot(keys[:, span], queries, preferred_element_type=jnp.float32)
            scores = jnp.where(mask, scores, MASKED)
            old = peak[request, head : head + 1, :]
            new = jnp.maximum(old, jnp.max(scores, axis=0, keepdims=True))
            weight = jnp.exp(scores - new)
            fade = jnp.exp(old - new)
            peak[request, head : head + 1, :] = new
            total[request, head : head + 1, :] = total[request, head : head + 1, :] * fade + jnp.sum(
                weight, axis=0, keepdims=True
            )
            term = lax.dot_general(
                values[:, span], weight.astype(jnp.bfloat16), (((0,), (0,)), ((), ())),
                preferred_element_type=jnp.float32,
            )
            acc[request, span, :] = acc[request, span, :] * fade + term

    own_rows = nk_ref.shape[0]
    key_at = lax.broadcasted_iota(jnp.int32, (own_rows, width), 0) + first_ref[1]
    query_at = lax.broadcasted_iota(jnp.int32, (own_rows, width), 1)
    step(first_ref[0], nk_ref[...], nv_ref[...], key_at <= query_at)

    slot_at = lax.broadcasted_iota(jnp.int32, (slots, width), 0)

    def one_block(block, carry):
        @pl.when(bound_ref[block] > 0)
        def _():
            step(owner_ref[block], k_ref[block], v_ref[block], slot_at < bound_ref[block])

        return carry

    lax.fori_loop(0, blocks, one_block, 0)

    for request in range(requests):
        for c in range(per_request):
            chunk = slice(c * rows, (c + 1) * rows)
            where_to = place_ref[request * per_request + c]
            out_ref[where_to] = acc[request, :, chunk].astype(jnp.bfloat16)
            stat_ref[where_to, 0] = jnp.concatenate(
                [peak[request, :, chunk], total[request, :, chunk]], axis=0
            )


def attend(owner, bound, place, first, queries, keys, values, new_keys, new_values, requests, head_dim):
    seq, feats, rows = queries.shape
    blocks, slots = keys.shape[:2]
    span = GROUP * head_dim
    groups = feats // span
    per_request = seq // requests
    own_rows = new_keys.shape[0]
    width = per_request * rows
    work = (blocks + 1) * slots * width * feats * 4
    return pl.pallas_call(
        functools.partial(
            attend_kernel, requests=requests, per_request=per_request, head_dim=head_dim
        ),
        grid_spec=pltpu.PrefetchScalarGridSpec(
            num_scalar_prefetch=4,
            grid=(groups,),
            in_specs=[
                pl.BlockSpec((seq, span, rows), lambda g, *_: (0, g, 0)),
                pl.BlockSpec((blocks, slots, span), lambda g, *_: (0, 0, g)),
                pl.BlockSpec((blocks, slots, span), lambda g, *_: (0, 0, g)),
                pl.BlockSpec((own_rows, span), lambda g, *_: (0, g)),
                pl.BlockSpec((own_rows, span), lambda g, *_: (0, g)),
            ],
            out_specs=[
                pl.BlockSpec((seq, span, rows), lambda g, *_: (0, g, 0)),
                pl.BlockSpec((seq, 1, 2 * GROUP, rows), lambda g, *_: (0, g, 0, 0)),
            ],
            scratch_shapes=[
                pltpu.VMEM((requests, span, width), jnp.float32),
                pltpu.VMEM((requests, GROUP, width), jnp.float32),
                pltpu.VMEM((requests, GROUP, width), jnp.float32),
            ],
        ),
        out_shape=[
            jax.ShapeDtypeStruct((seq, feats, rows), jnp.bfloat16),
            jax.ShapeDtypeStruct((seq, groups, 2 * GROUP, rows), jnp.float32),
        ],
        compiler_params=pltpu.CompilerParams(vmem_limit_bytes=48 * 1024 * 1024),
        cost_estimate=pl.CostEstimate(
            flops=8 * work, bytes_accessed=4 * queries.size + 4 * keys.size,
            transcendentals=work // (4 * head_dim),
        ),
    )(owner, bound, place, first, queries, keys, values, new_keys, new_values)


def merge(part_a, part_b, head_dim):
    out_a, stat_a = part_a
    out_b, stat_b = part_b
    count, groups, _, rows = stat_a.shape
    peak_a, peak_b = stat_a[:, :, :GROUP], stat_b[:, :, :GROUP]
    top = jnp.maximum(peak_a, peak_b)
    fade_a, fade_b = jnp.exp(peak_a - top), jnp.exp(peak_b - top)
    total = stat_a[:, :, GROUP:] * fade_a + stat_b[:, :, GROUP:] * fade_b
    shape = (count, groups, GROUP, head_dim, rows)
    out = (
        out_a.reshape(shape).astype(jnp.float32) * fade_a[:, :, :, None]
        + out_b.reshape(shape).astype(jnp.float32) * fade_b[:, :, :, None]
    )
    return out, top, total


def reduce_halves(out, stat, seq, head_dim):
    bit = 1
    while bit < seq:
        half = out.shape[0] // 2
        swap = [(i, i ^ bit) for i in range(seq)]
        came_out = lax.ppermute(out[half:], "seq", swap)
        came_stat = lax.ppermute(stat[half:], "seq", swap)
        merged, top, total = merge((out[:half], stat[:half]), (came_out, came_stat), head_dim)
        bit *= 2
        if bit < seq:
            out = merged.astype(jnp.bfloat16).reshape((half,) + out.shape[1:])
            stat = jnp.concatenate([top, total], axis=2)
    return merged[0] / total[0][:, :, None]


def local(features, gain, w_qkv, rope_factors, cache_len, cache_kv, block_owner, block_base):
    rows = features.shape[0]
    seq = lax.axis_size("seq")
    me = lax.axis_index("seq")
    wide_x = lax.all_gather(features, "tensor", axis=1, tiled=True).astype(jnp.float32)
    normed = (
        wide_x * lax.rsqrt(jnp.mean(wide_x * wide_x, axis=1, keepdims=True) + EPSILON) * gain
    ).astype(jnp.bfloat16)
    projected = jnp.einsum("td,dcf->cft", normed, w_qkv, preferred_element_type=jnp.float32)
    feats = projected.shape[1]
    head_dim = 2 * rope_factors.shape[0]
    heads = feats // head_dim
    requests = cache_len.shape[0]
    per_request = seq // requests
    request = me // per_request
    first_row = (me % per_request) * rows
    positions = cache_len[request] + first_row + jnp.arange(rows, dtype=jnp.int32)
    inv_freq = 1.0 / (
        rope_factors
        * jnp.power(10000.0, jnp.arange(rope_factors.shape[0], dtype=jnp.float32) * 2.0 / head_dim)
    )
    angles = inv_freq[None, :, None] * positions.astype(jnp.float32)[None, None, :]
    cosine, sine = jnp.cos(angles) * MSCALE, jnp.sin(angles) * MSCALE
    shaped = projected.reshape(3, heads, head_dim, rows)
    queries = (rotate_rows(shaped[0], cosine, sine) * head_dim ** (-0.5)).astype(jnp.bfloat16)
    new_keys = rotate_rows(shaped[1], cosine, sine).astype(jnp.bfloat16).reshape(feats, rows).T
    new_values = shaped[2].astype(jnp.bfloat16).reshape(feats, rows).T
    new_kv = jnp.stack([new_keys, new_values], axis=1)

    clamped = jnp.minimum(block_owner, requests - 1)
    bound = jnp.where(block_owner < requests, cache_len[clamped] - block_base, 0)
    place = jnp.zeros((seq,), jnp.int32)
    flipped = jnp.arange(seq, dtype=jnp.int32) ^ me
    bit = 1
    while bit < seq:
        place = place * 2 + (flipped // bit) % 2
        bit *= 2
    first = jnp.stack([request, first_row]).astype(jnp.int32)
    cache_keys, cache_values = cache_kv[:, :, 0], cache_kv[:, :, 1]
    queries = queries.reshape(feats, rows)

    groups = heads // GROUP
    parts = 2 if groups % 2 == 0 else 1
    wide = feats // parts
    gathered = [
        lax.all_gather(queries[i * wide : (i + 1) * wide], "seq", axis=0) for i in range(parts)
    ]
    results = []
    for i in range(parts):
        cols = slice(i * wide, (i + 1) * wide)
        out, stat = attend(
            clamped, bound, place, first, gathered[i],
            cache_keys[:, :, cols], cache_values[:, :, cols],
            new_keys[:, cols], new_values[:, cols], requests, head_dim,
        )
        results.append(reduce_halves(out, stat, seq, head_dim).reshape(wide, rows))
    attended = jnp.concatenate(results, axis=0).astype(jnp.bfloat16).T
    return (attended, new_kv)


def solution(mesh):
    in_specs = (
        P("seq", "tensor"),
        P(),
        P(None, None, "tensor"),
        P(),
        P(),
        P("seq", None, None, "tensor"),
        P("seq"),
        P("seq"),
    )
    out_specs = (P("seq", "tensor"), P("seq", None, "tensor"))
    return jax.shard_map(local, mesh=mesh, in_specs=in_specs, out_specs=out_specs, check_vma=False)
```

```python
import functools
import jax
import jax.numpy as jnp
from jax import lax
from jax.experimental import pallas as pl
from jax.experimental.pallas import tpu as pltpu
from jax.sharding import PartitionSpec as P

EPSILON = 1e-05
FLOOR = -1e30
MASKED = -2e30
MSCALE = 1.1902380714238083
GROUP = 4


def rotate_rows(vectors, cosine, sine):
    half = vectors.shape[1] // 2
    front, back = vectors[:, :half], vectors[:, half:]
    return jnp.concatenate([front * cosine - back * sine, back * cosine + front * sine], axis=1)


def attend_kernel(
    owner_ref, bound_ref, place_ref, first_ref,
    near_ref, far_ref, k_ref, v_ref, nk_ref, nv_ref,
    keep_ref, send_ref, keep_stat_ref, send_stat_ref, acc, peak, total,
    *, requests, pairs, head_dim,
):
    rows = near_ref.shape[2]
    blocks, slots = k_ref.shape[0], k_ref.shape[1]
    width = 2 * pairs * rows
    acc[...] = jnp.zeros_like(acc)
    peak[...] = jnp.full_like(peak, FLOOR)
    total[...] = jnp.zeros_like(total)

    def step(request, keys, values, mask):
        for head in range(GROUP):
            span = slice(head * head_dim, (head + 1) * head_dim)
            queries = jnp.concatenate(
                [ref[request * pairs + c, span, :] for ref in (near_ref, far_ref) for c in range(pairs)],
                axis=1,
            )
            scores = jnp.dot(keys[:, span], queries, preferred_element_type=jnp.float32)
            scores = jnp.where(mask, scores, MASKED)
            old = peak[request, head : head + 1, :]
            new = jnp.maximum(old, jnp.max(scores, axis=0, keepdims=True))
            weight = jnp.exp(scores - new)
            fade = jnp.exp(old - new)
            peak[request, head : head + 1, :] = new
            total[request, head : head + 1, :] = total[request, head : head + 1, :] * fade + jnp.sum(
                weight, axis=0, keepdims=True
            )
            term = lax.dot_general(
                values[:, span], weight.astype(jnp.bfloat16), (((0,), (0,)), ((), ())),
                preferred_element_type=jnp.float32,
            )
            acc[request, span, :] = acc[request, span, :] * fade + term

    own_rows = nk_ref.shape[0]
    key_at = lax.broadcasted_iota(jnp.int32, (own_rows, width), 0) + first_ref[1]
    lane = lax.broadcasted_iota(jnp.int32, (own_rows, rows), 1)
    query_at = jnp.concatenate(
        [lane + (2 * c + first_ref[2 + side]) * rows for side in range(2) for c in range(pairs)], axis=1
    )
    step(first_ref[0], nk_ref[...], nv_ref[...], key_at <= query_at)

    slot_at = lax.broadcasted_iota(jnp.int32, (slots, width), 0)

    def one_block(block, carry):
        @pl.when(bound_ref[block] > 0)
        def _():
            step(owner_ref[block], k_ref[block], v_ref[block], slot_at < bound_ref[block])

        return carry

    lax.fori_loop(0, blocks, one_block, 0)

    for request in range(requests):
        for c in range(2 * pairs):
            out_ref, stat_ref = ((keep_ref, keep_stat_ref), (send_ref, send_stat_ref))[c // pairs]
            chunk = slice(c * rows, (c + 1) * rows)
            where_to = place_ref[request * pairs + c % pairs]
            out_ref[where_to] = acc[request, :, chunk].astype(jnp.bfloat16)
            stat_ref[where_to, 0] = jnp.concatenate(
                [peak[request, :, chunk], total[request, :, chunk]], axis=0
            )


def attend(scalars, near, far, keys, values, new_keys, new_values, part, requests, head_dim):
    half, feats, rows = near.shape
    blocks, slots = keys.shape[:2]
    span = GROUP * head_dim
    groups = feats // span
    pairs = half // requests
    own_rows = new_keys.shape[0]
    width = 2 * pairs * rows
    work = (blocks + 1) * slots * width * feats
    base = part * groups
    return pl.pallas_call(
        functools.partial(attend_kernel, requests=requests, pairs=pairs, head_dim=head_dim),
        grid_spec=pltpu.PrefetchScalarGridSpec(
            num_scalar_prefetch=4,
            grid=(groups,),
            in_specs=[
                pl.BlockSpec((half, span, rows), lambda g, *_: (0, g, 0)),
                pl.BlockSpec((half, span, rows), lambda g, *_: (0, g, 0)),
                pl.BlockSpec((blocks, slots, span), lambda g, *_: (0, 0, base + g)),
                pl.BlockSpec((blocks, slots, span), lambda g, *_: (0, 0, base + g)),
                pl.BlockSpec((own_rows, span), lambda g, *_: (0, base + g)),
                pl.BlockSpec((own_rows, span), lambda g, *_: (0, base + g)),
            ],
            out_specs=[
                pl.BlockSpec((half, span, rows), lambda g, *_: (0, g, 0)),
                pl.BlockSpec((half, span, rows), lambda g, *_: (0, g, 0)),
                pl.BlockSpec((half, 1, 2 * GROUP, rows), lambda g, *_: (0, g, 0, 0)),
                pl.BlockSpec((half, 1, 2 * GROUP, rows), lambda g, *_: (0, g, 0, 0)),
            ],
            scratch_shapes=[
                pltpu.VMEM((requests, span, width), jnp.float32),
                pltpu.VMEM((requests, GROUP, width), jnp.float32),
                pltpu.VMEM((requests, GROUP, width), jnp.float32),
            ],
        ),
        out_shape=[jax.ShapeDtypeStruct((half, feats, rows), jnp.bfloat16)] * 2
        + [jax.ShapeDtypeStruct((half, groups, 2 * GROUP, rows), jnp.float32)] * 2,
        compiler_params=pltpu.CompilerParams(vmem_limit_bytes=40 * 1024 * 1024),
        cost_estimate=pl.CostEstimate(
            flops=16 * work, bytes_accessed=8 * near.size + 4 * keys.size,
            transcendentals=work // head_dim,
        ),
    )(*scalars, near, far, keys, values, new_keys, new_values)


def merge(part_a, part_b, head_dim):
    out_a, stat_a = part_a
    out_b, stat_b = part_b
    count, groups, _, rows = stat_a.shape
    peak_a, peak_b = stat_a[:, :, :GROUP], stat_b[:, :, :GROUP]
    top = jnp.maximum(peak_a, peak_b)
    fade_a, fade_b = jnp.exp(peak_a - top), jnp.exp(peak_b - top)
    total = stat_a[:, :, GROUP:] * fade_a + stat_b[:, :, GROUP:] * fade_b
    shape = (count, groups, GROUP, head_dim, rows)
    out = (
        out_a.reshape(shape).astype(jnp.float32) * fade_a[:, :, :, None]
        + out_b.reshape(shape).astype(jnp.float32) * fade_b[:, :, :, None]
    )
    return out, top, total


def swap(array, bit, seq):
    return lax.ppermute(array, "seq", [(i, i ^ bit) for i in range(seq)])


def exchange(keep, send, bit, seq, head_dim):
    came = (swap(send[0], bit, seq), swap(send[1], bit, seq))
    half = keep[0].shape[0] // 2

    def side(part):
        merged, top, total = merge((keep[0][part], keep[1][part]), (came[0][part], came[1][part]), head_dim)
        shape = (half,) + keep[0].shape[1:]
        return merged.astype(jnp.bfloat16).reshape(shape), jnp.concatenate([top, total], axis=2)

    send_next = side(slice(half, 2 * half))
    return side(slice(0, half)), send_next


def finish(keep, send, bit, seq, head_dim):
    while 2 * bit < seq:
        keep, send = exchange(keep, send, bit, seq, head_dim)
        bit *= 2
    came = (swap(send[0], bit, seq), swap(send[1], bit, seq))
    merged, _, total = merge(keep, came, head_dim)
    return merged[0] / total[0][:, :, None]


def local(features, gain, w_qkv, rope_factors, cache_len, cache_kv, block_owner, block_base):
    rows = features.shape[0]
    seq = lax.axis_size("seq")
    me = lax.axis_index("seq")
    wide_x = lax.all_gather(features, "tensor", axis=1, tiled=True)
    wide_x, cache_keys = lax.optimization_barrier((wide_x, cache_kv[:, :, 0]))
    wide_x = wide_x.astype(jnp.float32)
    normed = (
        wide_x * lax.rsqrt(jnp.mean(wide_x * wide_x, axis=1, keepdims=True) + EPSILON) * gain
    ).astype(jnp.bfloat16)
    normed, cache_late = lax.optimization_barrier((normed, cache_kv))
    projected = jnp.einsum("td,dcf->cft", normed, w_qkv, preferred_element_type=jnp.float32)
    feats = projected.shape[1]
    head_dim = 2 * rope_factors.shape[0]
    heads = feats // head_dim
    requests = cache_len.shape[0]
    per_request = seq // requests
    request = me // per_request
    first_row = (me % per_request) * rows
    positions = cache_len[request] + first_row + jnp.arange(rows, dtype=jnp.int32)
    inv_freq = 1.0 / (
        rope_factors
        * jnp.power(10000.0, jnp.arange(rope_factors.shape[0], dtype=jnp.float32) * 2.0 / head_dim)
    )
    angles = inv_freq[None, :, None] * positions.astype(jnp.float32)[None, None, :]
    cosine, sine = jnp.cos(angles) * MSCALE, jnp.sin(angles) * MSCALE
    shaped = projected.reshape(3, heads, head_dim, rows)
    queries = (rotate_rows(shaped[0], cosine, sine) * head_dim ** (-0.5)).astype(jnp.bfloat16)
    new_keys = rotate_rows(shaped[1], cosine, sine).astype(jnp.bfloat16).reshape(feats, rows).T
    new_values = shaped[2].astype(jnp.bfloat16).reshape(feats, rows).T
    new_kv = jnp.stack([new_keys, new_values], axis=1)

    clamped = jnp.minimum(block_owner, requests - 1)
    bound = jnp.where(block_owner < requests, cache_len[clamped] - block_base, 0)
    place = jnp.zeros((seq // 2,), jnp.int32)
    flipped = jnp.arange(seq // 2, dtype=jnp.int32) ^ (me // 2)
    bit = 1
    while bit < seq // 2:
        place = place * 2 + (flipped // bit) % 2
        bit *= 2
    side = me % 2
    first = jnp.stack([request, first_row, side, 1 - side]).astype(jnp.int32)
    scalars = (clamped, bound, place, first)
    cache_values = cache_late[:, :, 1]
    queries = queries.reshape(feats, rows)

    groups = heads // GROUP
    parts = 2 if groups % 2 == 0 else 1
    wide = feats // parts
    same_side = [list(range(core, seq, 2)) for core in range(2)]
    near = [
        lax.all_gather(queries[i * wide : (i + 1) * wide], "seq", axis=0, axis_index_groups=same_side)
        for i in range(parts)
    ]
    far = [swap(part, 1, seq) for part in near]
    states = []
    for i in range(parts):
        here, there = near[i], far[i]
        if states:
            states[-1], here, there = lax.optimization_barrier((states[-1], here, there))
        keep, send, keep_stat, send_stat = attend(
            scalars, here, there, cache_keys, cache_values, new_keys, new_values, i, requests, head_dim
        )
        states.append(exchange((keep, keep_stat), (send, send_stat), 1, seq, head_dim))
    results = [finish(keep, send, 2, seq, head_dim).reshape(wide, rows) for keep, send in states]
    attended = jnp.concatenate(results, axis=0).astype(jnp.bfloat16).T
    return (attended, new_kv)


def solution(mesh):
    in_specs = (
        P("seq", "tensor"),
        P(),
        P(None, None, "tensor"),
        P(),
        P(),
        P("seq", None, None, "tensor"),
        P("seq"),
        P("seq"),
    )
    out_specs = (P("seq", "tensor"), P("seq", None, "tensor"))
    return jax.shard_map(local, mesh=mesh, in_specs=in_specs, out_specs=out_specs, check_vma=False)
```

```python
import functools
import jax
import jax.numpy as jnp
from jax import lax
from jax.experimental import pallas as pl
from jax.experimental.pallas import tpu as pltpu
from jax.sharding import PartitionSpec as P

EPSILON = 1e-05
FLOOR = -1e30
MASKED = -2e30
MSCALE = 1.1902380714238083
GROUP = 4


def rotate_rows(vectors, cosine, sine):
    half = vectors.shape[1] // 2
    front, back = vectors[:, :half], vectors[:, half:]
    return jnp.concatenate([front * cosine - back * sine, back * cosine + front * sine], axis=1)


def attend_kernel(
    owner_ref, bound_ref, place_ref, first_ref,
    q_ref, k_ref, v_ref, nk_ref, nv_ref,
    keep_ref, send_ref, keep_stat_ref, send_stat_ref, acc, peak, total,
    *, requests, pairs, head_dim,
):
    rows = q_ref.shape[3]
    blocks, slots = k_ref.shape[0], k_ref.shape[1]
    width = 2 * pairs * rows
    acc[...] = jnp.zeros_like(acc)
    peak[...] = jnp.full_like(peak, FLOOR)
    total[...] = jnp.zeros_like(total)

    def step(request, keys, values, mask):
        for head in range(GROUP):
            span = slice(head * head_dim, (head + 1) * head_dim)
            queries = jnp.concatenate(
                [
                    q_ref[request * pairs + c, first_ref[2 + side], span, :]
                    for side in range(2)
                    for c in range(pairs)
                ],
                axis=1,
            )
            scores = jnp.dot(keys[:, span], queries, preferred_element_type=jnp.float32)
            scores = jnp.where(mask, scores, MASKED)
            old = peak[request, head : head + 1, :]
            new = jnp.maximum(old, jnp.max(scores, axis=0, keepdims=True))
            weight = jnp.exp(scores - new)
            fade = jnp.exp(old - new)
            peak[request, head : head + 1, :] = new
            total[request, head : head + 1, :] = total[request, head : head + 1, :] * fade + jnp.sum(
                weight, axis=0, keepdims=True
            )
            term = lax.dot_general(
                values[:, span], weight.astype(jnp.bfloat16), (((0,), (0,)), ((), ())),
                preferred_element_type=jnp.float32,
            )
            acc[request, span, :] = acc[request, span, :] * fade + term

    own_rows = nk_ref.shape[0]
    key_at = lax.broadcasted_iota(jnp.int32, (own_rows, width), 0) + first_ref[1]
    lane = lax.broadcasted_iota(jnp.int32, (own_rows, rows), 1)
    query_at = jnp.concatenate(
        [lane + (2 * c + first_ref[2 + side]) * rows for side in range(2) for c in range(pairs)], axis=1
    )
    step(first_ref[0], nk_ref[...], nv_ref[...], key_at <= query_at)

    slot_at = lax.broadcasted_iota(jnp.int32, (slots, width), 0)

    def one_block(block, carry):
        @pl.when(bound_ref[block] > 0)
        def _():
            step(owner_ref[block], k_ref[block], v_ref[block], slot_at < bound_ref[block])

        return carry

    lax.fori_loop(0, blocks, one_block, 0)

    for request in range(requests):
        for c in range(2 * pairs):
            out_ref, stat_ref = ((keep_ref, keep_stat_ref), (send_ref, send_stat_ref))[c // pairs]
            chunk = slice(c * rows, (c + 1) * rows)
            where_to = place_ref[request * pairs + c % pairs]
            out_ref[where_to] = acc[request, :, chunk].astype(jnp.bfloat16)
            stat_ref[where_to, 0] = jnp.concatenate(
                [peak[request, :, chunk], total[request, :, chunk]], axis=0
            )


def attend(scalars, queries, keys, values, new_keys, new_values, part, parts, requests, head_dim):
    half, _, feats, rows = queries.shape
    feats = feats // parts
    blocks, slots = keys.shape[:2]
    span = GROUP * head_dim
    groups = feats // span
    pairs = half // requests
    own_rows = new_keys.shape[0]
    width = 2 * pairs * rows
    work = (blocks + 1) * slots * width * feats
    base = part * groups
    return pl.pallas_call(
        functools.partial(attend_kernel, requests=requests, pairs=pairs, head_dim=head_dim),
        grid_spec=pltpu.PrefetchScalarGridSpec(
            num_scalar_prefetch=4,
            grid=(groups,),
            in_specs=[
                pl.BlockSpec((half, 2, span, rows), lambda g, *_: (0, 0, base + g, 0)),
                pl.BlockSpec((blocks, slots, span), lambda g, *_: (0, 0, base + g)),
                pl.BlockSpec((blocks, slots, span), lambda g, *_: (0, 0, base + g)),
                pl.BlockSpec((own_rows, span), lambda g, *_: (0, base + g)),
                pl.BlockSpec((own_rows, span), lambda g, *_: (0, base + g)),
            ],
            out_specs=[
                pl.BlockSpec((half, span, rows), lambda g, *_: (0, g, 0)),
                pl.BlockSpec((half, span, rows), lambda g, *_: (0, g, 0)),
                pl.BlockSpec((half, 1, 2 * GROUP, rows), lambda g, *_: (0, g, 0, 0)),
                pl.BlockSpec((half, 1, 2 * GROUP, rows), lambda g, *_: (0, g, 0, 0)),
            ],
            scratch_shapes=[
                pltpu.VMEM((requests, span, width), jnp.float32),
                pltpu.VMEM((requests, GROUP, width), jnp.float32),
                pltpu.VMEM((requests, GROUP, width), jnp.float32),
            ],
        ),
        out_shape=[jax.ShapeDtypeStruct((half, feats, rows), jnp.bfloat16)] * 2
        + [jax.ShapeDtypeStruct((half, groups, 2 * GROUP, rows), jnp.float32)] * 2,
        compiler_params=pltpu.CompilerParams(vmem_limit_bytes=40 * 1024 * 1024),
        cost_estimate=pl.CostEstimate(
            flops=16 * work, bytes_accessed=4 * queries.size + 4 * keys.size,
            transcendentals=work // head_dim,
        ),
    )(*scalars, queries, keys, values, new_keys, new_values)


def merge(part_a, part_b, head_dim):
    out_a, stat_a = part_a
    out_b, stat_b = part_b
    count, groups, _, rows = stat_a.shape
    peak_a, peak_b = stat_a[:, :, :GROUP], stat_b[:, :, :GROUP]
    top = jnp.maximum(peak_a, peak_b)
    fade_a, fade_b = jnp.exp(peak_a - top), jnp.exp(peak_b - top)
    total = stat_a[:, :, GROUP:] * fade_a + stat_b[:, :, GROUP:] * fade_b
    shape = (count, groups, GROUP, head_dim, rows)
    out = (
        out_a.reshape(shape).astype(jnp.float32) * fade_a[:, :, :, None]
        + out_b.reshape(shape).astype(jnp.float32) * fade_b[:, :, :, None]
    )
    return out, top, total


def swap(array, bit, seq):
    return lax.ppermute(array, "seq", [(i, i ^ bit) for i in range(seq)])


def exchange(keep, send, bit, seq, head_dim):
    came = (swap(send[0], bit, seq), swap(send[1], bit, seq))
    half = keep[0].shape[0] // 2

    def side(part):
        merged, top, total = merge((keep[0][part], keep[1][part]), (came[0][part], came[1][part]), head_dim)
        shape = (half,) + keep[0].shape[1:]
        return merged.astype(jnp.bfloat16).reshape(shape), jnp.concatenate([top, total], axis=2)

    send_next = side(slice(half, 2 * half))
    return side(slice(0, half)), send_next


def finish(keep, send, bit, seq, head_dim):
    while 2 * bit < seq:
        keep, send = exchange(keep, send, bit, seq, head_dim)
        bit *= 2
    came = (swap(send[0], bit, seq), swap(send[1], bit, seq))
    merged, _, total = merge(keep, came, head_dim)
    return merged[0] / total[0][:, :, None]


def local(features, gain, w_qkv, rope_factors, cache_len, cache_kv, block_owner, block_base):
    rows = features.shape[0]
    seq = lax.axis_size("seq")
    me = lax.axis_index("seq")
    wide_x = lax.all_gather(features, "tensor", axis=1, tiled=True)
    wide_x, cache_keys = lax.optimization_barrier((wide_x, cache_kv[:, :, 0]))
    wide_x = wide_x.astype(jnp.float32)
    normed = (
        wide_x * lax.rsqrt(jnp.mean(wide_x * wide_x, axis=1, keepdims=True) + EPSILON) * gain
    ).astype(jnp.bfloat16)
    normed, cache_late = lax.optimization_barrier((normed, cache_kv))
    projected = jnp.einsum("td,dcf->cft", normed, w_qkv, preferred_element_type=jnp.float32)
    feats = projected.shape[1]
    head_dim = 2 * rope_factors.shape[0]
    heads = feats // head_dim
    requests = cache_len.shape[0]
    per_request = seq // requests
    request = me // per_request
    first_row = (me % per_request) * rows
    positions = cache_len[request] + first_row + jnp.arange(rows, dtype=jnp.int32)
    inv_freq = 1.0 / (
        rope_factors
        * jnp.power(10000.0, jnp.arange(rope_factors.shape[0], dtype=jnp.float32) * 2.0 / head_dim)
    )
    angles = inv_freq[None, :, None] * positions.astype(jnp.float32)[None, None, :]
    cosine, sine = jnp.cos(angles) * MSCALE, jnp.sin(angles) * MSCALE
    shaped = projected.reshape(3, heads, head_dim, rows)
    queries = (rotate_rows(shaped[0], cosine, sine) * head_dim ** (-0.5)).astype(jnp.bfloat16)
    new_keys = rotate_rows(shaped[1], cosine, sine).astype(jnp.bfloat16).reshape(feats, rows).T
    new_values = shaped[2].astype(jnp.bfloat16).reshape(feats, rows).T
    new_kv = jnp.stack([new_keys, new_values], axis=1)

    clamped = jnp.minimum(block_owner, requests - 1)
    bound = jnp.where(block_owner < requests, cache_len[clamped] - block_base, 0)
    place = jnp.zeros((seq // 2,), jnp.int32)
    flipped = jnp.arange(seq // 2, dtype=jnp.int32) ^ (me // 2)
    bit = 1
    while bit < seq // 2:
        place = place * 2 + (flipped // bit) % 2
        bit *= 2
    side = me % 2
    first = jnp.stack([request, first_row, side, 1 - side]).astype(jnp.int32)
    scalars = (clamped, bound, place, first)
    cache_values = cache_late[:, :, 1]
    queries = queries.reshape(feats, rows)

    groups = heads // GROUP
    parts = 2 if groups % 2 == 0 else 1
    wide = feats // parts
    gathered = lax.all_gather(queries, "seq", axis=0).reshape(seq // 2, 2, feats, rows)
    states = []
    for i in range(parts):
        here = gathered
        if states:
            states[-1], here = lax.optimization_barrier((states[-1], here))
        keep, send, keep_stat, send_stat = attend(
            scalars, here, cache_keys, cache_values, new_keys, new_values, i, parts, requests, head_dim
        )
        states.append(exchange((keep, keep_stat), (send, send_stat), 1, seq, head_dim))
    results = [finish(keep, send, 2, seq, head_dim).reshape(wide, rows) for keep, send in states]
    attended = jnp.concatenate(results, axis=0).astype(jnp.bfloat16).T
    return (attended, new_kv)


def solution(mesh):
    in_specs = (
        P("seq", "tensor"),
        P(),
        P(None, None, "tensor"),
        P(),
        P(),
        P("seq", None, None, "tensor"),
        P("seq"),
        P("seq"),
    )
    out_specs = (P("seq", "tensor"), P("seq", None, "tensor"))
    return jax.shard_map(local, mesh=mesh, in_specs=in_specs, out_specs=out_specs, check_vma=False)
```
